256 devices in a mesh: pipe: 32 (over x, z_hi, core), expert: 8 (over y, z_lo).
Axes of the slice: x: 4, y: 4, z: 8 (z_hi: 4, z_lo: 2; z = z_hi * 2 + z_lo), core: 2. Of those that a mesh axis runs over, the one named last changes fastest.
Arguments:
- tokens: bfloat16 [32768, 3584], P(('pipe', 'expert')), may hold values from -6 to 6
- routes: int32 [32768, 2], P(('pipe', 'expert')), may hold values from 0 to 31, all different within a row; in each aligned block of 128 rows (0 to 127, 128 to 255, ...) at most 10 rows name the same one
- route_weight: float32 [32768, 2], P(('pipe', 'expert')), may hold values from 0.2 to 1
- w_gate: bfloat16 [32, 3584, 2048], P('pipe', None, 'expert'), may hold values from -0.09375 to 0.09375
- w_up: bfloat16 [32, 3584, 2048], P('pipe', None, 'expert'), may hold values from -0.09375 to 0.09375
- w_down: bfloat16 [32, 3584, 2048], P('pipe', None, 'expert'), may hold values from -0.125 to 0.125
Outputs:
- combined: bfloat16 [32768, 3584], P(('pipe', 'expert'))
The draws below stay inside these ranges and needn't reach their ends.
Inputs may be any that keep to these rules, and one draw needn't show every extreme that they name: `routes`: within the rows of one device (aligned blocks of 128 rows) the 2 entries of a row differ, and no expert is named more than 10 times; some expert is named exactly 10 times in some block.
All inputs are finite; a program needn't handle non-finite values.
Results may differ from the reference program's by a relative error of at most 0.017.
Values may be sent and summed in bfloat16 or wider, within the bound.
A program may use at most 128 MiB of HBM per device.

```python
import math
import jax
import jax.numpy as jnp
import numpy as np
from jax import lax

D = 3584
FF = 2048
TOP = 2
TOK_DEV = 128
EXPERTS = 32
FF_DEV = 256
CAP = 10
TOKENS = 32768
N_EXPERT = 8


def block_levels(key, extent, shards, smallest, largest):
    factor_of = 1.0
    for dim, parts in shards:
        heights = jax.random.uniform(jax.random.fold_in(jax.random.fold_in(key, 6), dim), (parts,), jnp.float32, smallest / len(shards), largest / len(shards))
        factor_of = factor_of * jnp.repeat(jnp.exp(heights), extent[dim] // parts).reshape((-1,) + (1,) * (len(extent) - 1 - dim))
    return factor_of


def routed_block(key, own, number, rows, number_of, top, reach, lean):
    ranking = jax.random.permutation(key, number_of)
    heavy_load, usual = portions_of(number_of, rows * top, reach, lean, True), portions_of(number_of, rows * top, reach, lean, False)
    places = jnp.arange(number_of)

    def named(tallies, offset_by):
        used = int((tallies > 0).sum())
        fixed = max(1, used // 4)
        shifted = fixed + (places - fixed + offset_by * (used - fixed)) % max(1, number_of - fixed)
        return jnp.zeros((number_of,), jnp.int32).at[ranking[jnp.where(places < fixed, places, shifted)]].set(jnp.asarray(tallies, jnp.int32))

    tallies = jnp.where(number % 4 == 0, named(heavy_load, number // 4), named(usual, number - number // 4 - 1))
    mixed = jax.random.permutation(jax.random.fold_in(own, 3), number_of)
    giver, sink = mixed[0:number_of // 2 * 2:2], mixed[1:number_of // 2 * 2:2]
    room = jnp.minimum(tallies[giver] - 1, reach - tallies[sink]) // 2
    room = jnp.where((giver == ranking[0]) | (sink == ranking[0]) | (tallies[sink] == 0), 0, jnp.maximum(room, 0))
    shifted = jax.random.randint(jax.random.fold_in(own, 4), (number_of // 2,), 0, 1 << 20) % (room + 1)
    tallies = tallies.at[giver].add(-shifted).at[sink].add(shifted)
    labels = jnp.searchsorted(jnp.cumsum(tallies), jnp.arange(rows * top), side="right").astype(jnp.int32)
    grid = labels.reshape(top, rows).T
    grid = grid[jax.random.permutation(jax.random.fold_in(own, 1), rows)]
    offset_by = jax.random.randint(jax.random.fold_in(own, 2), (rows, 1), 0, top)
    return jnp.take_along_axis(grid, (jnp.arange(top)[None, :] + offset_by) % top, axis=1)


def portions_of(amount, total, limit, lean, full):
    weights = [(1 << 20) // math.isqrt(grade ** lean) + 1 for grade in range(1, amount + 1)]
    largest = limit if full else min(limit, max(-(-total // amount), total * weights[0] // sum(weights)))
    least = 1 if total - largest >= amount - 1 else 0
    counts, rest = [largest] + [least] * (amount - 1), total - largest - least * (amount - 1)
    while rest > 0:
        candidates = [i for i in range(1, amount) if counts[i] < largest] or [i for i in range(1, amount) if counts[i] < limit]
        mass, budget = sum([weights[i] for i in candidates]), rest
        for i in candidates:
            extra = min(limit - counts[i], max(1, budget * weights[i] // mass), rest)
            counts[i] = counts[i] + extra
            rest = rest - extra
    return np.array(counts)


def gaussian(rng, extent, scale, limit, cuts=(), kind=jnp.bfloat16):
    entries = scale * jax.random.normal(rng, extent, jnp.float32)
    if cuts:
        entries = entries * block_levels(rng, extent, cuts, -0.22, 0.18)
    return jnp.clip(entries, -limit, limit).astype(kind)


def setup_inputs(seed: int = 0) -> dict:
    streams_of = jax.random.split(jax.random.key(seed), 7)
    tokens = gaussian(streams_of[0], (TOKENS, D), 1.0, 6.0, ((0, 256),))
    routes_keys = jax.random.split(jax.random.fold_in(streams_of[1], 1), TOKENS // TOK_DEV)
    routes_turns = jax.random.permutation(jax.random.fold_in(streams_of[1], 3), TOKENS // TOK_DEV)
    routes = jax.vmap(lambda own, number: routed_block(jax.random.fold_in(streams_of[1], 2), own, number, TOK_DEV, EXPERTS, TOP, CAP, 2))(routes_keys, routes_turns).reshape((TOKENS, TOP))
    route_weight = jnp.clip(0.2 + 0.8 * jax.random.uniform(streams_of[2], (TOKENS, TOP), jnp.float32) ** block_levels(streams_of[2], (TOKENS, TOP), ((0, 256),), -0.2, 0.2), 0.2, 1.0)
    w_gate = gaussian(streams_of[3], (EXPERTS, D, FF), D ** -0.5, 0.09375, ((0, 32), (2, 8)))
    w_up = gaussian(streams_of[4], (EXPERTS, D, FF), D ** -0.5, 0.09375, ((0, 32), (2, 8)))
    w_down = gaussian(streams_of[5], (EXPERTS, D, FF), FF ** -0.5, 0.125, ((0, 32), (2, 8)))
    return {"tokens": tokens, "routes": routes, "route_weight": route_weight, "w_gate": w_gate, "w_up": w_up, "w_down": w_down}


def slot_numbers(routes):
    blocks = routes.reshape(-1, TOK_DEV * TOP)
    onehot = (blocks[:, :, None] == jnp.arange(EXPERTS, dtype=jnp.int32)[None, None, :]).astype(jnp.int32)
    before = jnp.cumsum(onehot, axis=1) - onehot
    return jnp.sum(before * onehot, axis=2).reshape(-1).astype(jnp.int32)


def expert_apply(rows_in, gate_w, up_w, down_w):
    gate_proj = jnp.dot(rows_in, gate_w, preferred_element_type=jnp.float32)
    up_proj = jnp.dot(rows_in, up_w, preferred_element_type=jnp.float32)
    hidden = (jax.nn.silu(gate_proj) * up_proj).astype(jnp.bfloat16)
    running = jnp.zeros((rows_in.shape[0], D), jnp.float32)
    for group_id in range(N_EXPERT):
        lower = group_id * FF_DEV
        partial_value = jnp.dot(hidden[:, lower:lower + FF_DEV], down_w[:, lower:lower + FF_DEV].T, preferred_element_type=jnp.float32)
        running = running + lax.optimization_barrier(partial_value.astype(jnp.bfloat16)).astype(jnp.float32)
    return running.astype(jnp.bfloat16)


def reference(tokens, routes, route_weight, w_gate, w_up, w_down):
    num_blocks = TOKENS // TOK_DEV
    total_slots = num_blocks * CAP
    flat_routes = routes.reshape(-1)
    flat_weight = route_weight.reshape(-1)
    slot_index = slot_numbers(routes)
    pair_index = jnp.arange(TOKENS * TOP, dtype=jnp.int32)
    block_index = pair_index // (TOK_DEV * TOP)
    token_index = pair_index // TOP
    position = block_index * CAP + slot_index

    def one_expert(combined, inputs):
        gate_w, up_w, down_w, expert_id = inputs
        chosen = flat_routes == expert_id
        target = jnp.where(chosen, position, total_slots).astype(jnp.int32)
        slot_table = jnp.full((total_slots,), TOKENS, jnp.int32).at[target].set(token_index, mode="drop")
        slot_weight = jnp.zeros((total_slots,), jnp.float32).at[target].set(flat_weight, mode="drop")
        rows_in = tokens[jnp.minimum(slot_table, TOKENS - 1)]
        outputs = expert_apply(rows_in, gate_w, up_w, down_w)
        weighted = outputs.astype(jnp.float32) * slot_weight[:, None]
        combined = combined.at[slot_table].add(weighted, mode="drop")
        return combined, None

    start_sum = jnp.zeros((TOKENS, D), jnp.float32)
    combined, _ = lax.scan(one_expert, start_sum, (w_gate, w_up, w_down, jnp.arange(EXPERTS, dtype=jnp.int32)))
    return combined.astype(jnp.bfloat16)
```

```python
import functools

import jax
import jax.numpy as jnp
from jax import lax
from jax.experimental import pallas as pl
from jax.experimental.pallas import tpu as pltpu
from jax.sharding import PartitionSpec as P

MESH = pl.DeviceIdType.MESH
BF = jnp.bfloat16
F32 = jnp.float32
NX, NH, NY = 4, 4, 4
NC = 7
SLOTS = 10


def mm(a, b):
    return jnp.dot(a, b, preferred_element_type=F32)


def mm_nt(a, b):
    return lax.dot_general(a, b, (((1,), (1,)), ((), ())), preferred_element_type=F32)


def iota(shape, dim):
    return lax.broadcasted_iota(jnp.int32, shape, dim).astype(F32)


def kernel(
    tok, info, wg, wu, wd, out,
    stok, sinfo, wgu, wdn, xs, xr, zs, rows, rows2, acc, hid, own, pr, yr, ur, cs, cr, co,
    perm, disp, comb,
    w_rs, w_sw, w_ys, w_ss, t_s, t_r, x_s, x_r, z_s, z_r, y_s, y_r,
    py_s, py_r, rz_s, rz_r, rx_s, rx_r, c_s, c_r,
):
    pipe, expert = lax.axis_index("pipe"), lax.axis_index("expert")
    c, zh, x = pipe % 2, (pipe // 2) % NH, pipe // (2 * NH)
    zl, y = expert % 2, expert // 2
    ch = wgu.shape[3]
    nrow = perm.shape[0]
    same = c == zl

    def dev(x_, zh_, c_, y_, zl_):
        return ((x_ * NH + zh_) * 2 + c_, y_ * 2 + zl_)

    sib = dev(x, zh, 1 - c, y, zl)
    swap = dev(x, zh, 1 - c, y, 1 - zl)
    y_w = dev(x, zh, c, y + 1 - 2 * (y % 2), zl)
    y_c = dev(x, zh, c, NY - 1 - y, zl)

    def xdev(j):
        return dev((x + j) % NX, zh, c, y, zl)

    def zdev(j):
        return dev(x, (zh + j) % NH, zl, y, c)

    def rcopy(src, dst, ss, rs, to):
        return pltpu.make_async_remote_copy(
            src_ref=src, dst_ref=dst, send_sem=ss, recv_sem=rs, device_id=to, device_id_type=MESH
        )

    barrier = pltpu.get_barrier_semaphore()

    def greet(to):
        pl.semaphore_signal(barrier, inc=1, device_id=to, device_id_type=MESH)

    for to in [sib, y_w, y_c] + [xdev(j) for j in (1, 2, 3)] + [zdev(j) for j in (1, 2, 3)]:
        greet(to)

    @pl.when(jnp.logical_not(same))
    def _():
        greet(swap)

    pl.semaphore_wait(barrier, 9 + jnp.where(same, 0, 1))

    def piece(k, m):
        at = pl.ds(pl.multiple_of(k * ch, ch), ch)
        return (wg, wu, wd)[m].at[0, at, :]

    def held(s, k, m):
        return wdn.at[s, k] if m == 2 else wgu.at[s, k, m]

    def own_local(k, m):
        return pltpu.make_async_copy(piece(k, m), held(0, k, m), w_rs.at[0, k, m])

    def own_swap(k, m):
        return rcopy(piece(k, m), held(0, k, m), w_sw.at[k, m], w_rs.at[0, k, m], swap)

    def to_y(src, k, m):
        return rcopy(src, held(1, k, m), w_ys.at[k, m], w_rs.at[1, k, m], y_w)

    def to_sib(src, s, k, m):
        return rcopy(src, held(s, k, m), w_ss.at[s - 2, k, m], w_rs.at[s, k, m], sib)

    def start_own(k, m):
        @pl.when(same)
        def _():
            own_local(k, m).start()
            to_y(piece(k, m), k, m).start()
            to_sib(piece(k, m), 2, k, m).start()

        @pl.when(jnp.logical_not(same))
        def _():
            own_swap(k, m).start()

    def relay_held(k, m):
        @pl.when(same)
        def _():
            own_local(k, m).wait()

        @pl.when(jnp.logical_not(same))
        def _():
            own_swap(k, m).wait_recv()
            to_y(held(0, k, m), k, m).start()
            to_sib(held(0, k, m), 2, k, m).start()

    def relay_y(k, m):
        to_y(held(0, k, m), k, m).wait_recv()
        to_sib(held(1, k, m), 3, k, m).start()

    def wait_sib(k, m):
        for s in (2, 3):
            to_sib(held(s - 2, k, m), s, k, m).wait_recv()

    def wait_weight_sends(k, m):
        to_y(held(0, k, m), k, m).wait_send()
        to_sib(held(0, k, m), 2, k, m).wait_send()
        to_sib(held(1, k, m), 3, k, m).wait_send()

        @pl.when(jnp.logical_not(same))
        def _():
            own_swap(k, m).wait_send()

    def x_copy(src, dst, ss, rs, k, j):
        return rcopy(src.at[k, (x + j) % NX], dst.at[k, x], ss.at[k, j], rs.at[k, j], xdev(j))

    def x_land(src, dst, ss, rs, k, j):
        return rcopy(src.at[k, x], dst.at[k, (x + NX - j) % NX], ss.at[k, j], rs.at[k, j], xdev(j))

    def x_start(src, dst, ss, rs, k):
        for j in (1, 2, 3):
            x_copy(src, dst, ss, rs, k, j).start()
        dst[k, x] = src[k, x]

    def x_wait(src, dst, ss, rs, k):
        for j in (1, 2, 3):
            x_land(src, dst, ss, rs, k, j).wait_recv()

    def x_sent(src, dst, ss, rs, k):
        for j in (1, 2, 3):
            x_copy(src, dst, ss, rs, k, j).wait_send()

    def z_copy(src, dst, ss, rs, k, j):
        return rcopy(src.at[k, (zh + j) % NH], dst.at[k, zh], ss.at[k, j], rs.at[k, j], zdev(j))

    def z_land(src, dst, ss, rs, k, j):
        return rcopy(src.at[k, zh], dst.at[k, (zh + NH - j) % NH], ss.at[k, j], rs.at[k, j], zdev(j))

    def z_start(src, dst, ss, rs, k):
        for j in (1, 2, 3):
            z_copy(src, dst, ss, rs, k, j).start()

        @pl.when(same)
        def _():
            dst[k, zh] = src[k, zh]

        @pl.when(jnp.logical_not(same))
        def _():
            z_copy(src, dst, ss, rs, k, 0).start()

    def z_wait(src, dst, ss, rs, k):
        for j in (1, 2, 3):
            z_land(src, dst, ss, rs, k, j).wait_recv()

        @pl.when(jnp.logical_not(same))
        def _():
            z_land(src, dst, ss, rs, k, 0).wait_recv()

    def z_sent(src, dst, ss, rs, k):
        for j in (1, 2, 3):
            z_copy(src, dst, ss, rs, k, j).wait_send()

        @pl.when(jnp.logical_not(same))
        def _():
            z_copy(src, dst, ss, rs, k, 0).wait_send()

    def flat(ref, k):
        return ref[k].reshape(nrow, ch)

    def blocks(v):
        return v.astype(BF).reshape(4, nrow // 4, ch)

    def loop(n, body):
        def step(i, carry):
            body(i)
            return carry

        lax.fori_loop(0, n, step, 0)

    def lagged(i, lag, fn):
        k = i - lag

        @pl.when(jnp.logical_and(k >= 0, k < NC))
        def _():
            fn(k)

    tok_copy = rcopy(tok, stok, t_s.at[0], t_r.at[0], sib)
    info_copy = rcopy(info, sinfo, t_s.at[1], t_r.at[1], sib)
    info_copy.start()
    tok_copy.start()

    def first_weights(k):
        start_own(k, 0)
        start_own(k, 1)

    loop(NC, first_weights)

    n_tok = tok.shape[0]
    cf = c.astype(F32)

    def targets(route, slot, sc):
        chip = jnp.floor(route * 0.5)
        parity = route - 2.0 * chip
        return jnp.where(parity == cf, chip * (2 * SLOTS) + sc * SLOTS + slot, -1.0)

    def build(side, table, sc):
        r0, r1, g0, g1 = (table[i : i + 1, :] for i in range(4))
        experts = 2 * NX * NH
        e = iota((experts, n_tok), 0)
        m0 = jnp.where(e == r0, 1.0, 0.0)
        m1 = jnp.where(e == r1, 1.0, 0.0)
        earlier = jnp.where(iota((n_tok, n_tok), 0) < iota((n_tok, n_tok), 1), 1.0, 0.0)
        before = mm((m0 + m1).astype(BF), earlier.astype(BF))
        t0 = targets(r0, jnp.sum(before * m0, axis=0, keepdims=True), sc)
        t1 = targets(r1, jnp.sum(before * m1, axis=0, keepdims=True), sc)
        r = iota((nrow, n_tok), 0)
        h0 = jnp.where(r == t0, 1.0, 0.0)
        h1 = jnp.where(r == t1, 1.0, 0.0)
        disp[side] = (h0 + h1).astype(BF)
        weight = h0 * g0 + h1 * g1
        high = weight.astype(BF)
        comb[side, 0] = high
        comb[side, 1] = (weight - high.astype(F32)).astype(BF)

    build(0, info[...], cf)
    o = iota((nrow, nrow), 0)
    i_ = iota((nrow, nrow), 1)
    part = nrow // 16
    a = jnp.floor((o + 0.5) * (1.0 / (4 * part)))
    b = jnp.floor((o - 4 * part * a + 0.5) * (1.0 / part))
    rest = o - 4 * part * a - part * b
    perm[...] = jnp.where(i_ == b * (4 * part) + a * part + rest, 1.0, 0.0).astype(BF)

    info_copy.wait_recv()
    build(1, sinfo[...], 1.0 - cf)
    tok_copy.wait_recv()

    def send_x(k):
        at = pl.ds(pl.multiple_of(k * ch, ch), ch)
        xs[k] = blocks(mm(disp[0], tok[:, at]) + mm(disp[1], stok[:, at]))
        x_start(xs, xr, x_s, x_r, k)

    loop(NC, send_x)

    def send_z(k):
        x_wait(xs, xr, x_s, x_r, k)
        zs[k] = blocks(mm(perm[...], flat(xr, k)))
        z_start(zs, rows, z_s, z_r, k)

    loop(NC, send_z)

    def cross(k):
        return rcopy(rows.at[k], rows2.at[k], y_s.at[k], y_r.at[k], y_c)

    def send_cross(k):
        z_wait(zs, rows, z_s, z_r, k)
        cross(k).start()

    def gate_up(k):
        cross(k).wait_recv()
        for m in (0, 1):
            wait_sib(k, m)

        def one(s):
            for m in (0, 1):
                w = wgu[s, k, m]
                for half, ref in ((0, rows), (1, rows2)):
                    p = mm(flat(ref, k), w)

                    @pl.when(k == 0)
                    def _(p=p, half=half, m=m):
                        acc[s, m, half] = p

                    @pl.when(k > 0)
                    def _(p=p, half=half, m=m):
                        acc[s, m, half] += p

        loop(4, one)

    def front(i):
        lagged(i, 0, send_cross)
        for m in (0, 1):
            lagged(i, 0, functools.partial(relay_held, m=m))
        lagged(i, 0, functools.partial(start_own, m=2))
        for m in (0, 1):
            lagged(i, 1, functools.partial(relay_y, m=m))
        lagged(i, 2, gate_up)

    loop(NC + 2, front)

    def activate(s):
        for half in (0, 1):
            g = acc[s, 0, half]
            hid[half, s] = (g / (1.0 + jnp.exp(-g)) * acc[s, 1, half]).astype(BF)

    loop(4, activate)

    def down(half, k):
        total = mm_nt(hid[half, 0], wdn[0, k])
        for s in (1, 2, 3):
            total = total + mm_nt(hid[half, s], wdn[s, k])
        return total

    def partial_copy(k):
        return rcopy(xr.at[k], pr.at[k], py_s.at[k], py_r.at[k], y_c)

    def send_partial(k):
        wait_sib(k, 2)
        xr[k] = blocks(down(1, k))
        partial_copy(k).start()
        own[k] = down(0, k)

    def send_back_z(k):
        partial_copy(k).wait_recv()
        z_sent(zs, rows, z_s, z_r, k)
        zs[k] = blocks(own[k] + flat(pr, k).astype(F32))
        z_start(zs, yr, rz_s, rz_r, k)

    def send_back_x(k):
        z_wait(zs, yr, rz_s, rz_r, k)
        x_sent(xs, xr, x_s, x_r, k)
        xs[k] = blocks(mm(perm[...], flat(yr, k)))
        x_start(xs, ur, rx_s, rx_r, k)

    def weighted(side, v):
        d = (((0,), (0,)), ((), ()))
        return lax.dot_general(
            comb[side, 0], v, d, preferred_element_type=F32
        ) + lax.dot_general(comb[side, 1], v, d, preferred_element_type=F32)

    def sum_copy(k):
        return rcopy(cs.at[k], cr.at[k], c_s.at[k], c_r.at[k], sib)

    def send_sum(k):
        x_wait(xs, ur, rx_s, rx_r, k)
        v = flat(ur, k)
        cs[k] = weighted(1, v).astype(BF)
        sum_copy(k).start()
        co[k] = weighted(0, v)

    def finish(k):
        sum_copy(k).wait_recv()
        at = pl.ds(pl.multiple_of(k * ch, ch), ch)
        out[:, at] = (co[k] + cr[k].astype(F32)).astype(BF)

    def back(i):
        lagged(i, 0, functools.partial(relay_held, m=2))
        lagged(i, 1, functools.partial(relay_y, m=2))
        lagged(i, 2, send_partial)
        lagged(i, 3, send_back_z)
        lagged(i, 5, send_back_x)
        lagged(i, 6, send_sum)
        lagged(i, 7, finish)

    loop(NC + 7, back)

    tok_copy.wait_send()
    info_copy.wait_send()

    def sent(k):
        for m in (0, 1, 2):
            wait_weight_sends(k, m)
        cross(k).wait_send()
        partial_copy(k).wait_send()
        z_sent(zs, yr, rz_s, rz_r, k)
        x_sent(xs, ur, rx_s, rx_r, k)
        sum_copy(k).wait_send()

    loop(NC, sent)


def on_device(tokens, routes, route_weight, w_gate, w_up, w_down):
    n_tok, width = tokens.shape
    ff = w_gate.shape[2]
    ch = width // NC
    nrow = NX * NH * 2 * SLOTS
    info = jnp.concatenate(
        [routes.astype(F32).T, route_weight.T, jnp.zeros((4, n_tok), F32)], axis=0
    )
    vm = pltpu.VMEM
    dma = pltpu.SemaphoreType.DMA
    grid4 = (NC, 4, nrow // 4, ch)
    vmem_spec = pl.BlockSpec(memory_space=pltpu.VMEM)
    any_spec = pl.BlockSpec(memory_space=pl.ANY)
    return pl.pallas_call(
        kernel,
        out_shape=jax.ShapeDtypeStruct((n_tok, width), BF),
        in_specs=[vmem_spec, vmem_spec, any_spec, any_spec, any_spec],
        out_specs=vmem_spec,
        scratch_shapes=[
            vm((n_tok, width), BF),
            vm((8, n_tok), F32),
            vm((4, NC, 2, ch, ff), BF),
            vm((4, NC, ch, ff), BF),
            vm(grid4, BF),
            vm(grid4, BF),
            vm(grid4, BF),
            vm(grid4, BF),
            vm(grid4, BF),
            vm((4, 2, 2, nrow, ff), F32),
            vm((2, 4, nrow, ff), BF),
            vm((NC, nrow, ch), F32),
            vm(grid4, BF),
            vm(grid4, BF),
            vm(grid4, BF),
            vm((NC, n_tok, ch), BF),
            vm((NC, n_tok, ch), BF),
            vm((NC, n_tok, ch), F32),
            vm((nrow, nrow), BF),
            vm((2, nrow, n_tok), BF),
            vm((2, 2, nrow, n_tok), BF),
            dma((4, NC, 3)),
            dma((NC, 3)),
            dma((NC, 3)),
            dma((2, NC, 3)),
            dma((2,)),
            dma((2,)),
            dma((NC, 4)),
            dma((NC, 4)),
            dma((NC, 4)),
            dma((NC, 4)),
            dma((NC,)),
            dma((NC,)),
            dma((NC,)),
            dma((NC,)),
            dma((NC, 4)),
            dma((NC, 4)),
            dma((NC, 4)),
            dma((NC, 4)),
            dma((NC,)),
            dma((NC,)),
        ],
        compiler_params=pltpu.CompilerParams(
            collective_id=0, has_side_effects=True, vmem_limit_bytes=63 * 2**20
        ),
    )(tokens, info, w_gate, w_up, w_down)


def solution(mesh):
    in_specs = (
        P(("pipe", "expert"), None),
        P(("pipe", "expert"), None),
        P(("pipe", "expert"), None),
        P("pipe", None, "expert"),
        P("pipe", None, "expert"),
        P("pipe", None, "expert"),
    )
    out_specs = P(("pipe", "expert"), None)
    return jax.shard_map(
        on_device, mesh=mesh, in_specs=in_specs, out_specs=out_specs, check_vma=False
    )
```

```python
import functools

import jax
import jax.numpy as jnp
from jax import lax
from jax.experimental import pallas as pl
from jax.experimental.pallas import tpu as pltpu
from jax.sharding import PartitionSpec as P

MESH = pl.DeviceIdType.MESH
BF = jnp.bfloat16
F32 = jnp.float32
NX, NH, NY = 4, 4, 4
NC = 7
SLOTS = 10
DOWN_AT = 7
X_AHEAD = 2


def mm(a, b):
    return jnp.dot(a, b, preferred_element_type=F32)


def mm_nt(a, b):
    return lax.dot_general(a, b, (((1,), (1,)), ((), ())), preferred_element_type=F32)


def iota(shape, dim):
    return lax.broadcasted_iota(jnp.int32, shape, dim).astype(F32)


def kernel(
    tok, routes, route_weight, wg, wu, wd, out,
    stok, info, sinfo, wgu, wdn, xs, xr, zs, rows, rows2, acc, hid, own, pr, yr, ur, cs, cr, co,
    perm, disp, comb,
    w_rs, w_sw, w_ys, w_ss, t_s, t_r, x_s, x_r, z_s, z_r, y_s, y_r,
    py_s, py_r, rz_s, rz_r, rx_s, rx_r, c_s, c_r,
):
    pipe, expert = lax.axis_index("pipe"), lax.axis_index("expert")
    c, zh, x = pipe % 2, (pipe // 2) % NH, pipe // (2 * NH)
    zl, y = expert % 2, expert // 2
    ch = wgu.shape[3]
    nrow = perm.shape[0]
    same = c == zl

    def dev(x_, zh_, c_, y_, zl_):
        return ((x_ * NH + zh_) * 2 + c_, y_ * 2 + zl_)

    sib = dev(x, zh, 1 - c, y, zl)
    swap = dev(x, zh, 1 - c, y, 1 - zl)
    y_w = dev(x, zh, c, y + 1 - 2 * (y % 2), zl)
    y_c = dev(x, zh, c, NY - 1 - y, zl)

    def xdev(j):
        return dev((x + j) % NX, zh, c, y, zl)

    def zdev(j):
        return dev(x, (zh + j) % NH, zl, y, c)

    def rcopy(src, dst, ss, rs, to):
        return pltpu.make_async_remote_copy(
            src_ref=src, dst_ref=dst, send_sem=ss, recv_sem=rs, device_id=to, device_id_type=MESH
        )

    barrier = pltpu.get_barrier_semaphore()

    def greet(to):
        pl.semaphore_signal(barrier, inc=1, device_id=to, device_id_type=MESH)

    for to in [sib, y_w, y_c] + [xdev(j) for j in (1, 2, 3)] + [zdev(j) for j in (1, 2, 3)]:
        greet(to)

    @pl.when(jnp.logical_not(same))
    def _():
        greet(swap)

    def piece(k, m):
        at = pl.ds(pl.multiple_of(k * ch, ch), ch)
        return (wg, wu, wd)[m].at[0, at, :]

    def held(s, k, m):
        return wdn.at[s, k] if m == 2 else wgu.at[s, k, m]

    def own_local(k, m):
        return pltpu.make_async_copy(piece(k, m), held(0, k, m), w_rs.at[0, k, m])

    def own_swap(k, m):
        return rcopy(piece(k, m), held(0, k, m), w_sw.at[k, m], w_rs.at[0, k, m], swap)

    def to_y(src, k, m):
        return rcopy(src, held(1, k, m), w_ys.at[k, m], w_rs.at[1, k, m], y_w)

    def to_sib(src, s, k, m):
        return rcopy(src, held(s, k, m), w_ss.at[s - 2, k, m], w_rs.at[s, k, m], sib)

    def start_own(k, m):
        @pl.when(same)
        def _():
            to_y(piece(k, m), k, m).start()

        @pl.when(jnp.logical_not(same))
        def _():
            own_swap(k, m).start()

    def start_own_near(k, m):
        @pl.when(same)
        def _():
            own_local(k, m).start()
            to_sib(piece(k, m), 2, k, m).start()

    def relay_held(k, m):
        @pl.when(same)
        def _():
            own_local(k, m).wait()

        @pl.when(jnp.logical_not(same))
        def _():
            own_swap(k, m).wait_recv()
            to_y(held(0, k, m), k, m).start()
            to_sib(held(0, k, m), 2, k, m).start()

    def relay_y(k, m):
        to_y(held(0, k, m), k, m).wait_recv()
        to_sib(held(1, k, m), 3, k, m).start()

    def wait_sib(k, m):
        for s in (2, 3):
            to_sib(held(s - 2, k, m), s, k, m).wait_recv()

    def wait_weight_sends(k, m):
        to_y(held(0, k, m), k, m).wait_send()
        to_sib(held(0, k, m), 2, k, m).wait_send()
        to_sib(held(1, k, m), 3, k, m).wait_send()

        @pl.when(jnp.logical_not(same))
        def _():
            own_swap(k, m).wait_send()

    def x_copy(src, dst, ss, rs, k, j):
        return rcopy(src.at[k, (x + j) % NX], dst.at[k, x], ss.at[k, j], rs.at[k, j], xdev(j))

    def x_land(src, dst, ss, rs, k, j):
        return rcopy(src.at[k, x], dst.at[k, (x + NX - j) % NX], ss.at[k, j], rs.at[k, j], xdev(j))

    def x_start(src, dst, ss, rs, k):
        for j in (1, 2, 3):
            x_copy(src, dst, ss, rs, k, j).start()
        dst[k, x] = src[k, x]

    def x_wait(src, dst, ss, rs, k):
        for j in (1, 2, 3):
            x_land(src, dst, ss, rs, k, j).wait_recv()

    def x_sent(src, dst, ss, rs, k):
        for j in (1, 2, 3):
            x_copy(src, dst, ss, rs, k, j).wait_send()

    def z_copy(src, dst, ss, rs, k, j):
        return rcopy(src.at[k, (zh + j) % NH], dst.at[k, zh], ss.at[k, j], rs.at[k, j], zdev(j))

    def z_land(src, dst, ss, rs, k, j):
        return rcopy(src.at[k, zh], dst.at[k, (zh + NH - j) % NH], ss.at[k, j], rs.at[k, j], zdev(j))

    def z_start(src, dst, ss, rs, k):
        for j in (1, 2, 3):
            z_copy(src, dst, ss, rs, k, j).start()

        @pl.when(same)
        def _():
            dst[k, zh] = src[k, zh]

        @pl.when(jnp.logical_not(same))
        def _():
            z_copy(src, dst, ss, rs, k, 0).start()

    def z_wait(src, dst, ss, rs, k):
        for j in (1, 2, 3):
            z_land(src, dst, ss, rs, k, j).wait_recv()

        @pl.when(jnp.logical_not(same))
        def _():
            z_land(src, dst, ss, rs, k, 0).wait_recv()

    def z_sent(src, dst, ss, rs, k):
        for j in (1, 2, 3):
            z_copy(src, dst, ss, rs, k, j).wait_send()

        @pl.when(jnp.logical_not(same))
        def _():
            z_copy(src, dst, ss, rs, k, 0).wait_send()

    def flat(ref, k):
        return ref[k].reshape(nrow, ch)

    def blocks(v):
        return v.astype(BF).reshape(4, nrow // 4, ch)

    def loop(n, body):
        def step(i, carry):
            body(i)
            return carry

        lax.fori_loop(0, n, step, 0)

    def lagged(i, lag, fn):
        k = i - lag

        @pl.when(jnp.logical_and(k >= 0, k < NC))
        def _():
            fn(k)

    def columns(k):
        return pl.ds(pl.multiple_of(k * ch, ch), ch)

    def tok_copy(k):
        at = columns(k)
        return rcopy(tok.at[:, at], stok.at[:, at], t_s.at[k], t_r.at[k], sib)

    n_tok = tok.shape[0]
    cf = c.astype(F32)

    def targets(route, slot, sc):
        chip = jnp.floor(route * 0.5)
        parity = route - 2.0 * chip
        return jnp.where(parity == cf, chip * (2 * SLOTS) + sc * SLOTS + slot, -1.0)

    def build(side, table, sc):
        r0, r1, g0, g1 = (table[i : i + 1, :] for i in range(4))
        experts = 2 * NX * NH
        e = iota((experts, n_tok), 0)
        m0 = jnp.where(e == r0, 1.0, 0.0)
        m1 = jnp.where(e == r1, 1.0, 0.0)
        earlier = jnp.where(iota((n_tok, n_tok), 0) < iota((n_tok, n_tok), 1), 1.0, 0.0)
        before = mm((m0 + m1).astype(BF), earlier.astype(BF))
        t0 = targets(r0, jnp.sum(before * m0, axis=0, keepdims=True), sc)
        t1 = targets(r1, jnp.sum(before * m1, axis=0, keepdims=True), sc)
        r = iota((nrow, n_tok), 0)
        h0 = jnp.where(r == t0, 1.0, 0.0)
        h1 = jnp.where(r == t1, 1.0, 0.0)
        disp[side] = (h0 + h1).astype(BF)
        weight = h0 * g0 + h1 * g1
        high = weight.astype(BF)
        comb[side, 0] = high
        comb[side, 1] = (weight - high.astype(F32)).astype(BF)

    diagonal = iota((n_tok, n_tok), 0) == iota((n_tok, n_tok), 1)

    def as_row(column):
        return jnp.sum(jnp.where(diagonal, column, 0.0), axis=0, keepdims=True)

    info[...] = jnp.zeros_like(info)
    for i in (0, 1):
        info[i : i + 1, :] = as_row(routes[:, i : i + 1].astype(F32))
        info[2 + i : 3 + i, :] = as_row(route_weight[:, i : i + 1])
    build(0, info[...], cf)
    o = iota((nrow, nrow), 0)
    i_ = iota((nrow, nrow), 1)
    part = nrow // 16
    a = jnp.floor((o + 0.5) * (1.0 / (4 * part)))
    b = jnp.floor((o - 4 * part * a + 0.5) * (1.0 / part))
    rest = o - 4 * part * a - part * b
    perm[...] = jnp.where(i_ == b * (4 * part) + a * part + rest, 1.0, 0.0).astype(BF)

    pl.semaphore_wait(barrier, 9 + jnp.where(same, 0, 1))
    info_copy = rcopy(info, sinfo, t_s.at[NC], t_r.at[NC], sib)
    info_copy.start()
    loop(NC, lambda k: tok_copy(k).start())

    def first_weights(k):
        start_own(k, 0)
        start_own(k, 1)

    loop(NC, first_weights)
    info_copy.wait_recv()
    build(1, sinfo[...], 1.0 - cf)

    def send_x(k):
        tok_copy(k).wait_recv()
        at = columns(k)
        xs[k] = blocks(mm(disp[0], tok[:, at]) + mm(disp[1], stok[:, at]))
        x_start(xs, xr, x_s, x_r, k)
        start_own_near(k, 0)
        start_own_near(k, 1)

    for k in range(X_AHEAD):
        send_x(k)

    def send_z(k):
        x_wait(xs, xr, x_s, x_r, k)
        zs[k] = blocks(mm(perm[...], flat(xr, k)))
        z_start(zs, rows, z_s, z_r, k)

    def cross(k):
        return rcopy(rows.at[k], rows2.at[k], y_s.at[k], y_r.at[k], y_c)

    def send_cross(k):
        z_wait(zs, rows, z_s, z_r, k)
        cross(k).start()

    def gate_up(k):
        cross(k).wait_recv()
        for m in (0, 1):
            wait_sib(k, m)

        def one(s):
            for m in (0, 1):
                w = wgu[s, k, m]
                for half, ref in ((0, rows), (1, rows2)):
                    p = mm(flat(ref, k), w)

                    @pl.when(k == 0)
                    def _(p=p, half=half, m=m):
                        acc[s, m, half] = p

                    @pl.when(k > 0)
                    def _(p=p, half=half, m=m):
                        acc[s, m, half] += p

        loop(4, one)

    def start_down(k):
        start_own(k, 2)
        start_own_near(k, 2)

    def front(i):
        lagged(i, -X_AHEAD, send_x)
        for m in (0, 1):
            lagged(i, 0, functools.partial(relay_held, m=m))
        lagged(i, 0, send_z)
        lagged(i, 2, send_cross)
        for m in (0, 1):
            lagged(i, 2, functools.partial(relay_y, m=m))
        for k in range(NC):

            @pl.when(i == DOWN_AT + k // 2)
            def _(k=k):
                start_down(k)

        lagged(i, 4, gate_up)

    loop(NC + 4, front)

    def activate(s):
        for half in (0, 1):
            g = acc[s, 0, half]
            hid[half, s] = (g / (1.0 + jnp.exp(-g)) * acc[s, 1, half]).astype(BF)

    relay_held(0, 2)
    relay_held(1, 2)
    relay_y(0, 2)
    loop(4, activate)
    relay_held(2, 2)
    relay_y(1, 2)

    def down(half, k):
        total = mm_nt(hid[half, 0], wdn[0, k])
        for s in (1, 2, 3):
            total = total + mm_nt(hid[half, s], wdn[s, k])
        return total

    def partial_copy(k):
        return rcopy(xr.at[k], pr.at[k], py_s.at[k], py_r.at[k], y_c)

    def send_partial(k):
        wait_sib(k, 2)
        xr[k] = blocks(down(1, k))
        partial_copy(k).start()
        own[k] = down(0, k)

    def send_back_z(k):
        partial_copy(k).wait_recv()
        z_sent(zs, rows, z_s, z_r, k)
        zs[k] = blocks(own[k] + flat(pr, k).astype(F32))
        z_start(zs, yr, rz_s, rz_r, k)

    def send_back_x(k):
        z_wait(zs, yr, rz_s, rz_r, k)
        x_sent(xs, xr, x_s, x_r, k)
        xs[k] = blocks(mm(perm[...], flat(yr, k)))
        x_start(xs, ur, rx_s, rx_r, k)

    def weighted(side, v):
        d = (((0,), (0,)), ((), ()))
        return lax.dot_general(
            comb[side, 0], v, d, preferred_element_type=F32
        ) + lax.dot_general(comb[side, 1], v, d, preferred_element_type=F32)

    def sum_copy(k):
        return rcopy(cs.at[k], cr.at[k], c_s.at[k], c_r.at[k], sib)

    def send_sum(k):
        x_wait(xs, ur, rx_s, rx_r, k)
        v = flat(ur, k)
        cs[k] = weighted(1, v).astype(BF)
        sum_copy(k).start()
        co[k] = weighted(0, v)

    def finish(k):
        sum_copy(k).wait_recv()
        at = columns(k)
        out[:, at] = (co[k] + cr[k].astype(F32)).astype(BF)

    def back(i):
        lagged(i, 0, send_partial)
        lagged(i, -3, functools.partial(relay_held, m=2))
        lagged(i, -2, functools.partial(relay_y, m=2))
        lagged(i, 1, send_back_z)
        lagged(i, 3, send_back_x)
        lagged(i, 4, send_sum)
        lagged(i, 5, finish)

    loop(NC + 5, back)

    info_copy.wait_send()
    loop(NC, lambda k: tok_copy(k).wait_send())

    def sent(k):
        for m in (0, 1, 2):
            wait_weight_sends(k, m)
        cross(k).wait_send()
        partial_copy(k).wait_send()
        z_sent(zs, yr, rz_s, rz_r, k)
        x_sent(xs, ur, rx_s, rx_r, k)
        sum_copy(k).wait_send()

    loop(NC, sent)


def on_device(tokens, routes, route_weight, w_gate, w_up, w_down):
    n_tok, width = tokens.shape
    ff = w_gate.shape[2]
    ch = width // NC
    nrow = NX * NH * 2 * SLOTS
    vm = pltpu.VMEM
    dma = pltpu.SemaphoreType.DMA
    grid4 = (NC, 4, nrow // 4, ch)
    vmem_spec = pl.BlockSpec(memory_space=pltpu.VMEM)
    any_spec = pl.BlockSpec(memory_space=pl.ANY)
    return pl.pallas_call(
        kernel,
        out_shape=jax.ShapeDtypeStruct((n_tok, width), BF),
        in_specs=[vmem_spec] * 3 + [any_spec] * 3,
        out_specs=vmem_spec,
        scratch_shapes=[
            vm((n_tok, width), BF),
            vm((8, n_tok), F32),
            vm((8, n_tok), F32),
            vm((4, NC, 2, ch, ff), BF),
            vm((4, NC, ch, ff), BF),
            vm(grid4, BF),
            vm(grid4, BF),
            vm(grid4, BF),
            vm(grid4, BF),
            vm(grid4, BF),
            vm((4, 2, 2, nrow, ff), F32),
            vm((2, 4, nrow, ff), BF),
            vm((NC, nrow, ch), F32),
            vm(grid4, BF),
            vm(grid4, BF),
            vm(grid4, BF),
            vm((NC, n_tok, ch), BF),
            vm((NC, n_tok, ch), BF),
            vm((NC, n_tok, ch), F32),
            vm((nrow, nrow), BF),
            vm((2, nrow, n_tok), BF),
            vm((2, 2, nrow, n_tok), BF),
            dma((4, NC, 3)),
            dma((NC, 3)),
            dma((NC, 3)),
            dma((2, NC, 3)),
            dma((NC + 1,)),
            dma((NC + 1,)),
            dma((NC, 4)),
            dma((NC, 4)),
            dma((NC, 4)),
            dma((NC, 4)),
            dma((NC,)),
            dma((NC,)),
            dma((NC,)),
            dma((NC,)),
            dma((NC, 4)),
            dma((NC, 4)),
            dma((NC, 4)),
            dma((NC, 4)),
            dma((NC,)),
            dma((NC,)),
        ],
        compiler_params=pltpu.CompilerParams(
            collective_id=0, has_side_effects=True, vmem_limit_bytes=63 * 2**20
        ),
    )(tokens, routes, route_weight, w_gate, w_up, w_down)


def solution(mesh):
    in_specs = (
        P(("pipe", "expert"), None),
        P(("pipe", "expert"), None),
        P(("pipe", "expert"), None),
        P("pipe", None, "expert"),
        P("pipe", None, "expert"),
        P("pipe", None, "expert"),
    )
    out_specs = P(("pipe", "expert"), None)
    return jax.shard_map(
        on_device, mesh=mesh, in_specs=in_specs, out_specs=out_specs, check_vma=False
    )
```

```python
import functools

import jax
import jax.numpy as jnp
from jax import lax
from jax.experimental import pallas as pl
from jax.experimental.pallas import tpu as pltpu
from jax.sharding import PartitionSpec as P

MESH = pl.DeviceIdType.MESH
BF = jnp.bfloat16
F32 = jnp.float32
NX, NH, NY = 4, 4, 4
NC = 7
SLOTS = 10
DOWN_AT = 7
X_AHEAD = 2


def mm(a, b):
    return jnp.dot(a, b, preferred_element_type=F32)


def mm_nt(a, b):
    return lax.dot_general(a, b, (((1,), (1,)), ((), ())), preferred_element_type=F32)


def iota(shape, dim):
    return lax.broadcasted_iota(jnp.int32, shape, dim).astype(F32)


def kernel(
    tok, routes, route_weight, wg, wu, wd, out,
    stok, info, sinfo, wgu, wdn, xs, xr, zs, rows, rows2, acc, hid, own, pr, yr, ur, cs, cr, co,
    perm, disp, comb,
    w_rs, w_sw, w_ys, w_ss, t_s, t_r, x_s, x_r, z_s, z_r, y_s, y_r,
    py_s, py_r, rz_s, rz_r, rx_s, rx_r, c_s, c_r,
):
    pipe, expert = lax.axis_index("pipe"), lax.axis_index("expert")
    c, zh, x = pipe % 2, (pipe // 2) % NH, pipe // (2 * NH)
    zl, y = expert % 2, expert // 2
    ch = wgu.shape[3]
    nrow = perm.shape[0]
    same = c == zl

    def dev(x_, zh_, c_, y_, zl_):
        return ((x_ * NH + zh_) * 2 + c_, y_ * 2 + zl_)

    sib = dev(x, zh, 1 - c, y, zl)
    swap = dev(x, zh, 1 - c, y, 1 - zl)
    y_w = dev(x, zh, c, y + 1 - 2 * (y % 2), zl)
    y_c = dev(x, zh, c, NY - 1 - y, zl)

    def xdev(j):
        return dev((x + j) % NX, zh, c, y, zl)

    def zdev(j):
        return dev(x, (zh + j) % NH, zl, y, c)

    def rcopy(src, dst, ss, rs, to):
        return pltpu.make_async_remote_copy(
            src_ref=src, dst_ref=dst, send_sem=ss, recv_sem=rs, device_id=to, device_id_type=MESH
        )

    barrier = pltpu.get_barrier_semaphore()

    def greet(to):
        pl.semaphore_signal(barrier, inc=1, device_id=to, device_id_type=MESH)

    for to in [sib, y_w, y_c] + [xdev(j) for j in (1, 2, 3)] + [zdev(j) for j in (1, 2, 3)]:
        greet(to)

    @pl.when(jnp.logical_not(same))
    def _():
        greet(swap)

    def piece(k, m):
        at = pl.ds(pl.multiple_of(k * ch, ch), ch)
        return (wg, wu, wd)[m].at[0, at, :]

    def held(s, k, m):
        return wdn.at[s, k] if m == 2 else wgu.at[s, k, m]

    def own_local(k, m):
        return pltpu.make_async_copy(piece(k, m), held(0, k, m), w_rs.at[0, k, m])

    def own_swap(k, m):
        return rcopy(piece(k, m), held(0, k, m), w_sw.at[k, m], w_rs.at[0, k, m], swap)

    def to_y(src, k, m):
        return rcopy(src, held(1, k, m), w_ys.at[k, m], w_rs.at[1, k, m], y_w)

    def to_sib(src, s, k, m):
        return rcopy(src, held(s, k, m), w_ss.at[s - 2, k, m], w_rs.at[s, k, m], sib)

    def start_own(k, m):
        @pl.when(same)
        def _():
            to_y(piece(k, m), k, m).start()

        @pl.when(jnp.logical_not(same))
        def _():
            own_swap(k, m).start()

    def start_own_near(k, m):
        @pl.when(same)
        def _():
            own_local(k, m).start()
            to_sib(piece(k, m), 2, k, m).start()

    def relay_held(k, m):
        @pl.when(same)
        def _():
            own_local(k, m).wait()

        @pl.when(jnp.logical_not(same))
        def _():
            own_swap(k, m).wait_recv()
            to_y(held(0, k, m), k, m).start()
            to_sib(held(0, k, m), 2, k, m).start()

    def relay_y(k, m):
        to_y(held(0, k, m), k, m).wait_recv()
        to_sib(held(1, k, m), 3, k, m).start()

    def wait_sib(k, m):
        for s in (2, 3):
            to_sib(held(s - 2, k, m), s, k, m).wait_recv()

    def pair_y(k):
        return rcopy(wgu.at[0, k], wgu.at[1, k], w_ys.at[k, 0], w_rs.at[1, k, 0], y_w)

    def pair_sib(s, k):
        return rcopy(wgu.at[s - 2, k], wgu.at[s, k], w_ss.at[s - 2, k, 0], w_rs.at[s, k, 0], sib)

    def relay_pair(k):
        @pl.when(same)
        def _():
            own_local(k, 0).wait()
            own_local(k, 1).wait()

        @pl.when(jnp.logical_not(same))
        def _():
            own_swap(k, 0).wait_recv()
            own_swap(k, 1).wait_recv()
            pair_y(k).start()
            pair_sib(2, k).start()

    def relay_pair_y(k):
        @pl.when(same)
        def _():
            to_y(held(0, k, 0), k, 0).wait_recv()
            to_y(held(0, k, 1), k, 1).wait_recv()

        @pl.when(jnp.logical_not(same))
        def _():
            pair_y(k).wait_recv()

        pair_sib(3, k).start()

    def wait_pair(k):
        @pl.when(same)
        def _():
            pair_sib(2, k).wait_recv()

        @pl.when(jnp.logical_not(same))
        def _():
            to_sib(held(0, k, 0), 2, k, 0).wait_recv()
            to_sib(held(0, k, 1), 2, k, 1).wait_recv()

        pair_sib(3, k).wait_recv()

    def wait_pair_sends(k):
        @pl.when(same)
        def _():
            for m in (0, 1):
                to_y(held(0, k, m), k, m).wait_send()
                to_sib(held(0, k, m), 2, k, m).wait_send()

        @pl.when(jnp.logical_not(same))
        def _():
            pair_y(k).wait_send()
            pair_sib(2, k).wait_send()
            own_swap(k, 0).wait_send()
            own_swap(k, 1).wait_send()

        pair_sib(3, k).wait_send()

    def wait_weight_sends(k, m):
        to_y(held(0, k, m), k, m).wait_send()
        to_sib(held(0, k, m), 2, k, m).wait_send()
        to_sib(held(1, k, m), 3, k, m).wait_send()

        @pl.when(jnp.logical_not(same))
        def _():
            own_swap(k, m).wait_send()

    def x_copy(src, dst, ss, rs, k, j):
        return rcopy(src.at[k, (x + j) % NX], dst.at[k, x], ss.at[k, j], rs.at[k, j], xdev(j))

    def x_land(src, dst, ss, rs, k, j):
        return rcopy(src.at[k, x], dst.at[k, (x + NX - j) % NX], ss.at[k, j], rs.at[k, j], xdev(j))

    def x_start(src, dst, ss, rs, k):
        for j in (1, 2, 3):
            x_copy(src, dst, ss, rs, k, j).start()
        dst[k, x] = src[k, x]

    def x_wait(src, dst, ss, rs, k):
        for j in (1, 2, 3):
            x_land(src, dst, ss, rs, k, j).wait_recv()

    def x_sent(src, dst, ss, rs, k):
        for j in (1, 2, 3):
            x_copy(src, dst, ss, rs, k, j).wait_send()

    def z_copy(src, dst, ss, rs, k, j):
        return rcopy(src.at[k, (zh + j) % NH], dst.at[k, zh], ss.at[k, j], rs.at[k, j], zdev(j))

    def z_land(src, dst, ss, rs, k, j):
        return rcopy(src.at[k, zh], dst.at[k, (zh + NH - j) % NH], ss.at[k, j], rs.at[k, j], zdev(j))

    def z_start(src, dst, ss, rs, k):
        for j in (2, 1, 3):
            z_copy(src, dst, ss, rs, k, j).start()

        @pl.when(same)
        def _():
            dst[k, zh] = src[k, zh]

        @pl.when(jnp.logical_not(same))
        def _():
            z_copy(src, dst, ss, rs, k, 0).start()

    def z_wait(src, dst, ss, rs, k):
        for j in (1, 2, 3):
            z_land(src, dst, ss, rs, k, j).wait_recv()

        @pl.when(jnp.logical_not(same))
        def _():
            z_land(src, dst, ss, rs, k, 0).wait_recv()

    def z_sent(src, dst, ss, rs, k):
        for j in (1, 2, 3):
            z_copy(src, dst, ss, rs, k, j).wait_send()

        @pl.when(jnp.logical_not(same))
        def _():
            z_copy(src, dst, ss, rs, k, 0).wait_send()

    def flat(ref, k):
        return ref[k].reshape(nrow, ch)

    def blocks(v):
        return v.astype(BF).reshape(4, nrow // 4, ch)

    def loop(n, body):
        def step(i, carry):
            body(i)
            return carry

        lax.fori_loop(0, n, step, 0)

    def lagged(i, lag, fn):
        k = i - lag

        @pl.when(jnp.logical_and(k >= 0, k < NC))
        def _():
            fn(k)

    def columns(k):
        return pl.ds(pl.multiple_of(k * ch, ch), ch)

    def tok_copy(k):
        at = columns(k)
        return rcopy(tok.at[:, at], stok.at[:, at], t_s.at[k], t_r.at[k], sib)

    n_tok = tok.shape[0]
    cf = c.astype(F32)

    def targets(route, slot, sc):
        chip = jnp.floor(route * 0.5)
        parity = route - 2.0 * chip
        return jnp.where(parity == cf, chip * (2 * SLOTS) + sc * SLOTS + slot, -1.0)

    def build(side, table, sc):
        r0, r1, g0, g1 = (table[i : i + 1, :] for i in range(4))
        experts = 2 * NX * NH
        e = iota((experts, n_tok), 0)
        m0 = jnp.where(e == r0, 1.0, 0.0)
        m1 = jnp.where(e == r1, 1.0, 0.0)
        earlier = jnp.where(iota((n_tok, n_tok), 0) < iota((n_tok, n_tok), 1), 1.0, 0.0)
        before = mm((m0 + m1).astype(BF), earlier.astype(BF))
        t0 = targets(r0, jnp.sum(before * m0, axis=0, keepdims=True), sc)
        t1 = targets(r1, jnp.sum(before * m1, axis=0, keepdims=True), sc)
        r = iota((nrow, n_tok), 0)
        h0 = jnp.where(r == t0, 1.0, 0.0)
        h1 = jnp.where(r == t1, 1.0, 0.0)
        disp[side] = (h0 + h1).astype(BF)
        weight = h0 * g0 + h1 * g1
        high = weight.astype(BF)
        comb[side, 0] = high
        comb[side, 1] = (weight - high.astype(F32)).astype(BF)

    diagonal = iota((n_tok, n_tok), 0) == iota((n_tok, n_tok), 1)

    def as_row(column):
        return jnp.sum(jnp.where(diagonal, column, 0.0), axis=0, keepdims=True)

    info[...] = jnp.zeros_like(info)
    for i in (0, 1):
        info[i : i + 1, :] = as_row(routes[:, i : i + 1].astype(F32))
        info[2 + i : 3 + i, :] = as_row(route_weight[:, i : i + 1])
    build(0, info[...], cf)
    o = iota((nrow, nrow), 0)
    i_ = iota((nrow, nrow), 1)
    part = nrow // 16
    a = jnp.floor((o + 0.5) * (1.0 / (4 * part)))
    b = jnp.floor((o - 4 * part * a + 0.5) * (1.0 / part))
    rest = o - 4 * part * a - part * b
    perm[...] = jnp.where(i_ == b * (4 * part) + a * part + rest, 1.0, 0.0).astype(BF)

    pl.semaphore_wait(barrier, 9 + jnp.where(same, 0, 1))
    info_copy = rcopy(info, sinfo, t_s.at[NC], t_r.at[NC], sib)
    info_copy.start()

    def first_weights(k):
        start_own(k, 0)
        start_own(k, 1)

    first_weights(0)
    loop(NC, lambda k: tok_copy(k).start())
    loop(NC - 1, lambda k: first_weights(k + 1))
    info_copy.wait_recv()
    build(1, sinfo[...], 1.0 - cf)

    def send_x(k):
        tok_copy(k).wait_recv()
        at = columns(k)
        xs[k] = blocks(mm(disp[0], tok[:, at]) + mm(disp[1], stok[:, at]))
        x_start(xs, xr, x_s, x_r, k)
        start_own_near(k, 0)
        start_own_near(k, 1)

    for k in range(X_AHEAD):
        send_x(k)

    def send_z(k):
        x_wait(xs, xr, x_s, x_r, k)
        zs[k] = blocks(mm(perm[...], flat(xr, k)))
        z_start(zs, rows, z_s, z_r, k)

    def cross(k, j):
        at = (zh + NH - j) % NH
        return rcopy(rows.at[k, at], rows2.at[k, at], y_s.at[k, j], y_r.at[k, j], y_c)

    def send_cross(k):
        for j in (0, 1, 3, 2):
            if j:
                z_land(zs, rows, z_s, z_r, k, j).wait_recv()
            else:

                @pl.when(jnp.logical_not(same))
                def _():
                    z_land(zs, rows, z_s, z_r, k, 0).wait_recv()

            cross(k, j).start()

    def gate_up(k):
        wait_pair(k)
        for j in range(NH):
            cross(k, j).wait_recv()

        def one(s):
            for m in (0, 1):
                w = wgu[s, k, m]
                for half, ref in ((0, rows), (1, rows2)):
                    p = mm(flat(ref, k), w)

                    @pl.when(k == 0)
                    def _(p=p, half=half, m=m):
                        acc[s, m, half] = p

                    @pl.when(k > 0)
                    def _(p=p, half=half, m=m):
                        acc[s, m, half] += p

        loop(4, one)

    def start_down(k):
        start_own(k, 2)
        start_own_near(k, 2)

    def front(i):
        lagged(i, -X_AHEAD, send_x)
        lagged(i, 0, relay_pair)
        lagged(i, 0, send_z)
        lagged(i, 2, send_cross)
        lagged(i, 2, relay_pair_y)
        for k in range(NC):

            @pl.when(i == DOWN_AT + k // 2)
            def _(k=k):
                start_down(k)

        lagged(i, 4, gate_up)

    loop(NC + 4, front)

    def activate(half, s):
        g = acc[s, 0, half]
        hid[half, s] = (g / (1.0 + jnp.exp(-g)) * acc[s, 1, half]).astype(BF)

    relay_held(0, 2)
    relay_held(1, 2)
    relay_y(0, 2)
    loop(4, functools.partial(activate, 1))
    relay_held(2, 2)
    relay_y(1, 2)

    def down(half, k):
        total = mm_nt(hid[half, 0], wdn[0, k])
        for s in (1, 2, 3):
            total = total + mm_nt(hid[half, s], wdn[s, k])
        return total

    def partial_copy(k):
        return rcopy(xr.at[k], pr.at[k], py_s.at[k], py_r.at[k], y_c)

    def send_partial(k):
        wait_sib(k, 2)
        xr[k] = blocks(down(1, k))
        partial_copy(k).start()

    def send_back_z(k):
        z_sent(zs, rows, z_s, z_r, k)
        own[...] = down(0, k)
        partial_copy(k).wait_recv()
        zs[k] = blocks(own[...] + flat(pr, k).astype(F32))
        z_start(zs, yr, rz_s, rz_r, k)

    def send_back_x(k):
        z_wait(zs, yr, rz_s, rz_r, k)
        x_sent(xs, xr, x_s, x_r, k)
        xs[k] = blocks(mm(perm[...], flat(yr, k)))
        x_start(xs, ur, rx_s, rx_r, k)

    def weighted(side, v):
        d = (((0,), (0,)), ((), ()))
        return lax.dot_general(
            comb[side, 0], v, d, preferred_element_type=F32
        ) + lax.dot_general(comb[side, 1], v, d, preferred_element_type=F32)

    def sum_copy(k):
        return rcopy(cs.at[k], cr.at[k], c_s.at[k], c_r.at[k], sib)

    def send_sum(k):
        x_wait(xs, ur, rx_s, rx_r, k)
        v = flat(ur, k)
        cs[k] = weighted(1, v).astype(BF)
        sum_copy(k).start()
        co[k] = weighted(0, v)

    def finish(k):
        sum_copy(k).wait_recv()
        at = columns(k)
        out[:, at] = (co[k] + cr[k].astype(F32)).astype(BF)

    def back(i):
        lagged(i, 0, send_partial)

        @pl.when(i == 0)
        def _():
            loop(4, functools.partial(activate, 0))

        lagged(i, 1, send_back_z)
        lagged(i, 3, send_back_x)
        lagged(i, 4, send_sum)
        lagged(i, 5, finish)
        lagged(i, -3, functools.partial(relay_held, m=2))
        lagged(i, -2, functools.partial(relay_y, m=2))

    loop(NC + 5, back)

    info_copy.wait_send()
    loop(NC, lambda k: tok_copy(k).wait_send())

    def sent(k):
        wait_pair_sends(k)
        wait_weight_sends(k, 2)
        for j in range(NH):
            cross(k, j).wait_send()
        partial_copy(k).wait_send()
        z_sent(zs, yr, rz_s, rz_r, k)
        x_sent(xs, ur, rx_s, rx_r, k)
        sum_copy(k).wait_send()

    loop(NC, sent)


def on_device(tokens, routes, route_weight, w_gate, w_up, w_down):
    n_tok, width = tokens.shape
    ff = w_gate.shape[2]
    ch = width // NC
    nrow = NX * NH * 2 * SLOTS
    vm = pltpu.VMEM
    dma = pltpu.SemaphoreType.DMA
    grid4 = (NC, 4, nrow // 4, ch)
    vmem_spec = pl.BlockSpec(memory_space=pltpu.VMEM)
    any_spec = pl.BlockSpec(memory_space=pl.ANY)
    return pl.pallas_call(
        kernel,
        out_shape=jax.ShapeDtypeStruct((n_tok, width), BF),
        in_specs=[vmem_spec] * 3 + [any_spec] * 3,
        out_specs=vmem_spec,
        scratch_shapes=[
            vm((n_tok, width), BF),
            vm((8, n_tok), F32),
            vm((8, n_tok), F32),
            vm((4, NC, 2, ch, ff), BF),
            vm((4, NC, ch, ff), BF),
            vm(grid4, BF),
            vm(grid4, BF),
            vm(grid4, BF),
            vm(grid4, BF),
            vm(grid4, BF),
            vm((4, 2, 2, nrow, ff), F32),
            vm((2, 4, nrow, ff), BF),
            vm((nrow, ch), F32),
            vm(grid4, BF),
            vm(grid4, BF),
            vm(grid4, BF),
            vm((NC, n_tok, ch), BF),
            vm((NC, n_tok, ch), BF),
            vm((NC, n_tok, ch), F32),
            vm((nrow, nrow), BF),
            vm((2, nrow, n_tok), BF),
            vm((2, 2, nrow, n_tok), BF),
            dma((4, NC, 3)),
            dma((NC, 3)),
            dma((NC, 3)),
            dma((2, NC, 3)),
            dma((NC + 1,)),
            dma((NC + 1,)),
            dma((NC, 4)),
            dma((NC, 4)),
            dma((NC, 4)),
            dma((NC, 4)),
            dma((NC, 4)),
            dma((NC, 4)),
            dma((NC,)),
            dma((NC,)),
            dma((NC, 4)),
            dma((NC, 4)),
            dma((NC, 4)),
            dma((NC, 4)),
            dma((NC,)),
            dma((NC,)),
        ],
        compiler_params=pltpu.CompilerParams(
            collective_id=0, has_side_effects=True, vmem_limit_bytes=63 * 2**20
        ),
    )(tokens, routes, route_weight, w_gate, w_up, w_down)


def solution(mesh):
    in_specs = (
        P(("pipe", "expert"), None),
        P(("pipe", "expert"), None),
        P(("pipe", "expert"), None),
        P("pipe", None, "expert"),
        P("pipe", None, "expert"),
        P("pipe", None, "expert"),
    )
    out_specs = P(("pipe", "expert"), None)
    return jax.shard_map(
        on_device, mesh=mesh, in_specs=in_specs, out_specs=out_specs, check_vma=False
    )
```
